32 devices in a mesh: worker: 8 (over y, x, core), shard: 4 (over z).
Axes of the slice: x: 2, y: 2, z: 4, core: 2. Of those that a mesh axis runs over, the one named last changes fastest.
Arguments:
- momentum: float32 [8, 2097152], P('worker', 'shard'), may hold values from -6 to 6
- gradient: float32 [8, 2097152], P('worker', 'shard'), may hold values from -40 to 40
- weights: float32 [2097152], P('shard'), may hold values from -0.6 to 0.6
Outputs:
- new_momentum: float32 [8, 2097152], P('worker', 'shard')
- new_weights: float32 [2097152], P('shard')
The draws below stay inside these ranges and needn't reach their ends.
All inputs are finite; a program needn't handle non-finite values.
Results may differ from the reference program's by a relative error of at most 0.0003.
Values sent between devices are 32-bit elements; how exact they have to be, the bound alone decides.
No kernel may reach another device: no remote copies, remote signals or barrier semaphores. Data moves between devices by JAX's collectives and lax.ppermute only.
A program may use at most 64 MiB of HBM per device.

```python
import jax
import jax.numpy as jnp

WORKERS = 8
TRIM = 2
P_SIZE = 2097152


def draw_gradient(key, part):
    keys = jax.random.split(jax.random.fold_in(key, 7), 6)
    shape = (WORKERS, P_SIZE)
    honest = jax.random.normal(keys[2], shape, dtype=jnp.float32)
    share = 0.2
    sizes = jax.random.uniform(keys[3], shape, dtype=jnp.float32, minval=10.0, maxval=30.0)
    signs = jnp.where(jax.random.uniform(keys[4], (1, P_SIZE), dtype=jnp.float32) < 0.5, -1.0, 1.0)
    attack = jax.random.uniform(keys[5], shape, dtype=jnp.float32) < share
    result = jnp.where(attack, signs * sizes, honest)
    return jnp.clip(result, -40.0, 40.0).astype(jnp.float32)


def levels(stream_key, extent, pieces, least, largest):
    loudness, own = 1.0, jax.random.fold_in(stream_key, 6)
    for dim, blocks in pieces:
        draws = jnp.exp(jax.random.uniform(jax.random.fold_in(own, dim), (blocks,), jnp.float32, least / len(pieces), largest / len(pieces)))
        loudness = loudness * jnp.repeat(draws, extent[dim] // blocks).reshape([-1 if axis == dim else 1 for axis in range(len(extent))])
    return loudness


def bell_draw(key, shape, width, most, shards=(), kind=jnp.bfloat16):
    values = jax.random.normal(key, shape, jnp.float32) * width
    if len(shards) > 0:
        values = levels(key, shape, shards, -0.22, 0.18) * values
    return jnp.clip(values, min=-most, max=most).astype(kind)


def setup_inputs(seed: int = 0) -> dict:
    splits = jax.random.split(jax.random.key(seed), 4)
    return {
        "momentum": bell_draw(splits[0], (WORKERS, P_SIZE), 1.0, 6.0, ((0, 8), (1, 4)), jnp.float32),
        "gradient": draw_gradient(jax.random.fold_in(splits[3], 71), 0),
        "weights": bell_draw(splits[2], (P_SIZE,), 0.1, 0.6, ((0, 4),), jnp.float32),
    }


def reference(momentum, gradient, weights):
    new_momentum = 0.9 * momentum + gradient
    ordered = jnp.sort(new_momentum, axis=0)
    kept = ordered[TRIM:WORKERS - TRIM]
    trimmed = jnp.sum(kept, axis=0) / (WORKERS - 2 * TRIM)
    new_weights = weights - 0.1 * trimmed
    return new_momentum, new_weights
```

```python
import functools

import jax
import jax.numpy as jnp
from jax import lax
from jax.experimental import pallas as pl
from jax.experimental.pallas import tpu as pltpu
from jax.sharding import PartitionSpec as P

LANES = 128
CORES = 2
ANY = pl.BlockSpec(memory_space=pl.ANY)


def partner(worker, mask, count):
    if count & (count - 1) == 0:
        return worker ^ mask
    return (mask - worker) % count


def block_of(worker, count):
    chips = count // CORES
    return (worker % CORES) * chips + worker // CORES


def order_pair(values, low, high):
    former, latter = values[low], values[high]
    values[low] = jnp.minimum(former, latter)
    values[high] = jnp.maximum(former, latter)


def network(count):
    pairs = []
    span = 1
    while span < count:
        step = span
        while step >= 1:
            for first in range(step % span, count - step, 2 * step):
                for low in range(first, min(first + step, count - step)):
                    if low // (2 * span) == (low + step) // (2 * span):
                        pairs.append((low, low + step))
            step //= 2
        span *= 2
    return pairs


def kept_mean(values):
    values = list(values)
    count = len(values)
    trim = count // 4
    for low, high in network(count):
        order_pair(values, low, high)
    total = functools.reduce(jnp.add, values[trim : count - trim])
    return total / (count - 2 * trim)


def update_kernel(workers, masks, rows, m_ref, g_ref, u_ref, *rest):
    sends = rest[: len(masks)]
    m_buf, g_buf, in_sem, out_sem = rest[len(masks) :]
    me = lax.axis_index("worker")
    spans, loads = [], []
    for i, mask in enumerate(masks):
        start = pl.multiple_of(block_of(partner(me, mask, workers), workers) * rows, 8)
        span = pl.ds(start, rows)
        pair = [
            pltpu.make_async_copy(m_ref.at[span], m_buf.at[i], in_sem.at[2 * i]),
            pltpu.make_async_copy(g_ref.at[span], g_buf.at[i], in_sem.at[2 * i + 1]),
        ]
        for copy in pair:
            copy.start()
        spans.append(span)
        loads.append(pair)
    stores = []
    for i in range(len(masks)):
        for copy in loads[i]:
            copy.wait()
        g_buf[i] = 0.9 * m_buf[i] + g_buf[i]
        pair = [
            pltpu.make_async_copy(g_buf.at[i], sends[i], out_sem.at[2 * i]),
            pltpu.make_async_copy(g_buf.at[i], u_ref.at[spans[i]], out_sem.at[2 * i + 1]),
        ]
        for copy in pair:
            copy.start()
        stores += pair
    for copy in stores:
        copy.wait()


def update(momentum, gradient, workers, masks):
    rows = momentum.shape[0] // workers
    block = jax.ShapeDtypeStruct((rows, LANES), jnp.float32)
    out = pl.pallas_call(
        functools.partial(update_kernel, workers, masks, rows),
        out_shape=[jax.ShapeDtypeStruct(momentum.shape, jnp.float32)] + [block] * len(masks),
        in_specs=[ANY, ANY],
        out_specs=[ANY] + [ANY] * len(masks),
        scratch_shapes=[
            pltpu.VMEM((len(masks), rows, LANES), jnp.float32),
            pltpu.VMEM((len(masks), rows, LANES), jnp.float32),
            pltpu.SemaphoreType.DMA((2 * len(masks),)),
            pltpu.SemaphoreType.DMA((2 * len(masks),)),
        ],
        compiler_params=pltpu.CompilerParams(vmem_limit_bytes=16 << 20),
        name="update",
    )(momentum, gradient)
    return out[0], out[1:]


def trim_kernel(workers, rows, w_ref, *rest):
    blocks = rest[:workers]
    o_ref, w_buf, sem = rest[workers:]
    me = lax.axis_index("worker")
    start = pl.multiple_of(block_of(me, workers) * rows, 8)
    copy = pltpu.make_async_copy(w_ref.at[pl.ds(start, rows)], w_buf, sem)
    copy.start()
    copy.wait()
    step = 8 * max(1, 32 // workers)

    def one(i, carry):
        span = pl.ds(pl.multiple_of(i * step, step), step)
        mean = kept_mean([block[span] for block in blocks])
        o_ref[span] = w_buf[span] - 0.1 * mean
        return carry

    lax.fori_loop(0, rows // step, one, 0)


def trim(weights, blocks, workers):
    rows = blocks[0].shape[0]
    vmem = pl.BlockSpec(memory_space=pltpu.VMEM)
    return pl.pallas_call(
        functools.partial(trim_kernel, workers, rows),
        out_shape=jax.ShapeDtypeStruct((rows, LANES), jnp.float32),
        in_specs=[ANY] + [vmem] * workers,
        out_specs=vmem,
        scratch_shapes=[pltpu.VMEM((rows, LANES), jnp.float32), pltpu.SemaphoreType.DMA],
        compiler_params=pltpu.CompilerParams(vmem_limit_bytes=16 << 20),
        name="trim",
    )(weights, *blocks)


def place_kernel(workers, rows, *rest):
    blocks, o_ref, sem = rest[:workers], rest[workers], rest[workers + 1]
    me = lax.axis_index("worker")
    copies = []
    for mask, block in enumerate(blocks):
        start = pl.multiple_of(block_of(partner(me, mask, workers), workers) * rows, 8)
        copies.append(pltpu.make_async_copy(block, o_ref.at[pl.ds(start, rows)], sem.at[mask]))
        copies[-1].start()
    for copy in copies:
        copy.wait()


def place(blocks, workers):
    rows = blocks[0].shape[0]
    return pl.pallas_call(
        functools.partial(place_kernel, workers, rows),
        out_shape=jax.ShapeDtypeStruct((workers * rows, LANES), jnp.float32),
        in_specs=[ANY] * workers,
        out_specs=ANY,
        scratch_shapes=[pltpu.SemaphoreType.DMA((workers,))],
        compiler_params=pltpu.CompilerParams(vmem_limit_bytes=16 << 20),
        name="place",
    )(*blocks)


def hbm(x):
    return pltpu.with_memory_space_constraint(x, pltpu.HBM)


def body(momentum, gradient, weights):
    workers = lax.axis_size("worker")

    def swap(block, mask):
        pairs = [(w, partner(w, mask, workers)) for w in range(workers)]
        return lax.ppermute(block, "worker", pairs)

    masks = list(range(workers))
    updated, sends = update(
        hbm(momentum.reshape(-1, LANES)), hbm(gradient.reshape(-1, LANES)), workers, masks
    )
    blocks = [sends[m] if m == 0 else swap(sends[m], m) for m in masks]
    own = trim(hbm(weights.reshape(-1, LANES)), blocks, workers)
    mine = {m: own if m == 0 else swap(own, m) for m in range(0, workers, CORES)}
    theirs = {m + 1: swap(mine[m], 1) for m in mine}
    new_weights = place([(mine | theirs)[m] for m in masks], workers)
    return updated.reshape(momentum.shape), new_weights.reshape(weights.shape)


def solution(mesh):
    return jax.shard_map(
        body,
        mesh=mesh,
        in_specs=(P("worker", "shard"), P("worker", "shard"), P("shard")),
        out_specs=(P("worker", "shard"), P("shard")),
        check_vma=False,
    )
```

```python
import functools

import jax
import jax.numpy as jnp
from jax import lax
from jax.experimental import pallas as pl
from jax.experimental.pallas import tpu as pltpu
from jax.sharding import PartitionSpec as P

LANES = 128
DEPTH = 4
LATER = 2
CORES = 2


def cost(size):
    return pl.CostEstimate(flops=size, bytes_accessed=4 * size, transcendentals=0)


ANY = pl.BlockSpec(memory_space=pl.ANY)
VMEM = pl.BlockSpec(memory_space=pltpu.VMEM)


def turned(label, core, chips):
    bits = chips.bit_length() - 1
    second = sum(1 << (j + 1) % bits for j in range(bits) if label >> j & 1) if bits else 0
    return label + core * (second - label)


def other_chip(chip, label, core, chips):
    if chips & (chips - 1) == 0:
        return chip ^ turned(label, core, chips)
    return (label - chip) % chips


def target(worker, label, flip, count):
    chip, core = worker // CORES, worker % CORES
    core_there = core + flip * (1 - 2 * core)
    return CORES * other_chip(chip, label, core, count // CORES) + core_there


def origin(worker, label, flip, count):
    chip, core = worker // CORES, worker % CORES
    core_there = core + flip * (1 - 2 * core)
    return CORES * other_chip(chip, label, core_there, count // CORES) + core_there


def block_of(worker, count):
    chips = count // CORES
    return (worker % CORES) * chips + worker // CORES


def order_pair(values, low, high):
    former, latter = values[low], values[high]
    values[low] = jnp.minimum(former, latter)
    values[high] = jnp.maximum(former, latter)


def network(count):
    pairs = []
    span = 1
    while span < count:
        step = span
        while step >= 1:
            for first in range(step % span, count - step, 2 * step):
                for low in range(first, min(first + step, count - step)):
                    if low // (2 * span) == (low + step) // (2 * span):
                        pairs.append((low, low + step))
            step //= 2
        span *= 2
    return pairs


def kept_mean(values):
    values = list(values)
    count = len(values)
    trim = count // 4
    for low, high in network(count):
        order_pair(values, low, high)
    total = functools.reduce(jnp.add, values[trim : count - trim])
    return total / (count - 2 * trim)


def send_kernel(workers, routes, cuts, rows, deps, m_ref, g_ref, *rest):
    rest = rest[deps:]
    count = sum(len(cut) - 1 for cut in cuts)
    sends = rest[:count]
    m_buf, g_buf, sem = rest[count:]
    me = lax.axis_index("worker")
    loads = []
    for i, route in enumerate(routes):
        start = pl.multiple_of(block_of(target(me, *route, workers), workers) * rows, 8)
        span = pl.ds(start, rows)
        pair = [
            pltpu.make_async_copy(m_ref.at[span], m_buf.at[i], sem.at[2 * i]),
            pltpu.make_async_copy(g_ref.at[span], g_buf.at[i], sem.at[2 * i + 1]),
        ]
        for copy in pair:
            copy.start()
        loads.append(pair)
    at = 0
    for i, cut in enumerate(cuts):
        for copy in loads[i]:
            copy.wait()
        for low, high in zip(cut[:-1], cut[1:]):
            sends[at][...] = 0.9 * m_buf[i, low:high] + g_buf[i, low:high]
            at += 1


def send_blocks(momentum, gradient, workers, routes, cuts, deps, name):
    rows = momentum.shape[0] // workers
    sizes = [high - low for cut in cuts for low, high in zip(cut[:-1], cut[1:])]
    return pl.pallas_call(
        functools.partial(send_kernel, workers, routes, cuts, rows, len(deps)),
        out_shape=[jax.ShapeDtypeStruct((size, LANES), jnp.float32) for size in sizes],
        in_specs=[ANY] * (2 + len(deps)),
        out_specs=[VMEM] * len(sizes),
        scratch_shapes=[
            pltpu.VMEM((len(routes), rows, LANES), jnp.float32),
            pltpu.VMEM((len(routes), rows, LANES), jnp.float32),
            pltpu.SemaphoreType.DMA((2 * len(routes),)),
        ],
        compiler_params=pltpu.CompilerParams(vmem_limit_bytes=16 << 20),
        cost_estimate=cost(3 * LANES * sum(sizes)),
        name=name,
    )(momentum, gradient, *deps)


def update_kernel(workers, pieces, rows, deps, m_ref, g_ref, w_ref, *rest):
    u_ref, own_ref, m_buf, g_buf, in_sem, out_sem, own_sem = rest[deps:]
    size = own_ref.shape[0]
    start = pl.multiple_of(block_of(lax.axis_index("worker"), workers) * size, 8)
    loads, stores = [], []
    for i in range(pieces):
        span = pl.ds(i * rows, rows)
        loads.append(
            [
                pltpu.make_async_copy(m_ref.at[span], m_buf.at[i], in_sem.at[2 * i]),
                pltpu.make_async_copy(g_ref.at[span], g_buf.at[i], in_sem.at[2 * i + 1]),
            ]
        )
        stores.append(pltpu.make_async_copy(g_buf.at[i], u_ref.at[span], out_sem.at[i]))
        for copy in loads[i]:
            copy.start()
    own = pltpu.make_async_copy(w_ref.at[pl.ds(start, size)], own_ref, own_sem)
    own.start()
    for i in range(pieces):
        for copy in loads[i]:
            copy.wait()
        g_buf[i] = 0.9 * m_buf[i] + g_buf[i]
        stores[i].start()
    for copy in stores + [own]:
        copy.wait()


def update(momentum, gradient, weights, workers, pieces, deps):
    rows = momentum.shape[0] // pieces
    own = (weights.shape[0] // workers, LANES)
    return pl.pallas_call(
        functools.partial(update_kernel, workers, pieces, rows, len(deps)),
        out_shape=[
            jax.ShapeDtypeStruct(momentum.shape, jnp.float32),
            jax.ShapeDtypeStruct(own, jnp.float32),
        ],
        in_specs=[ANY] * (3 + len(deps)),
        out_specs=[ANY, VMEM],
        scratch_shapes=[
            pltpu.VMEM((pieces, rows, LANES), jnp.float32),
            pltpu.VMEM((pieces, rows, LANES), jnp.float32),
            pltpu.SemaphoreType.DMA((2 * pieces,)),
            pltpu.SemaphoreType.DMA((pieces,)),
            pltpu.SemaphoreType.DMA,
        ],
        compiler_params=pltpu.CompilerParams(vmem_limit_bytes=16 << 20),
        cost_estimate=cost(3 * momentum.size),
        name="update",
    )(momentum, gradient, weights, *deps)


def trim_kernel(size, starts, *rest):
    blocks, o_ref = rest[: len(starts)], rest[-1]
    step = 8 * max(1, 32 // (len(starts) - 1))

    def one(i, carry):
        at = pl.multiple_of(i * step, step)
        own, *values = [b[pl.ds(s + at, step)] for b, s in zip(blocks, starts)]
        o_ref[pl.ds(at, step)] = own - 0.1 * kept_mean(values)
        return carry

    lax.fori_loop(0, size // step, one, 0)


def trim(weights, blocks, low, high, deps, name):
    rows = weights.shape[0]
    size = high - low
    starts = [low if block.shape[0] == rows else 0 for block in [weights, *blocks]]
    return pl.pallas_call(
        functools.partial(trim_kernel, size, starts),
        out_shape=jax.ShapeDtypeStruct((size, LANES), jnp.float32),
        in_specs=[VMEM] * len(starts) + [ANY] * len(deps),
        out_specs=VMEM,
        compiler_params=pltpu.CompilerParams(vmem_limit_bytes=16 << 20),
        cost_estimate=cost((len(starts) + 1) * size * LANES),
        name=name,
    )(weights, *blocks, *deps)


def place_kernel(workers, rows, places, *rest):
    blocks, (o_ref, sem) = rest[: len(places)], rest[len(places) :]
    me = lax.axis_index("worker")
    copies = []
    for i, (block, (low, *route)) in enumerate(zip(blocks, places)):
        start = block_of(origin(me, *route, workers), workers) * rows + low
        there = o_ref.at[pl.ds(pl.multiple_of(start, 8), block.shape[0])]
        copies.append(pltpu.make_async_copy(block, there, sem.at[i]))
        copies[i].start()
    for copy in copies:
        copy.wait()


def place(blocks, workers, rows):
    return pl.pallas_call(
        functools.partial(place_kernel, workers, rows, list(blocks)),
        out_shape=jax.ShapeDtypeStruct((workers * rows, LANES), jnp.float32),
        in_specs=[ANY] * len(blocks),
        out_specs=ANY,
        scratch_shapes=[pltpu.SemaphoreType.DMA((len(blocks),))],
        compiler_params=pltpu.CompilerParams(vmem_limit_bytes=16 << 20),
        cost_estimate=cost(2 * LANES * workers * rows),
        name="place",
    )(*blocks.values())


def copy_kernel(from_ref, *rest):
    rest[-1][...] = from_ref[...]


def copied(block, deps):
    return pl.pallas_call(
        copy_kernel,
        out_shape=jax.ShapeDtypeStruct(block.shape, jnp.float32),
        in_specs=[VMEM] + [ANY] * len(deps),
        out_specs=VMEM,
        compiler_params=pltpu.CompilerParams(vmem_limit_bytes=16 << 20),
        cost_estimate=cost(2 * block.size),
        name="copied",
    )(block, *deps)


def gate_kernel(*refs):
    del refs


def gate(blocks, deps):
    return pl.pallas_call(
        gate_kernel,
        out_shape=[jax.ShapeDtypeStruct(b.shape, b.dtype) for b in blocks],
        in_specs=[ANY] * (len(blocks) + len(deps)),
        out_specs=[ANY] * len(blocks),
        input_output_aliases={i: i for i in range(len(blocks))},
        compiler_params=pltpu.CompilerParams(vmem_limit_bytes=1 << 20),
        name="gate",
    )(*blocks, *deps)


def in_hbm(array):
    return pltpu.with_memory_space_constraint(array.reshape(-1, LANES), pltpu.HBM)


def body(momentum, gradient, weights):
    workers = lax.axis_size("worker")
    chips = workers // CORES
    m, g, w = in_hbm(momentum), in_hbm(gradient), in_hbm(weights)
    rows = m.shape[0] // workers
    cut = [0, rows // 2, rows]
    parts = list(zip(cut[:-1], cut[1:]))
    queue = []

    def send(block, route, deps=()):
        if deps:
            (block,) = gate([block], list(deps))
        pairs = [(i, target(i, *route, workers)) for i in range(workers)]
        return lax.ppermute(block, "worker", pairs)

    def queued(block, route, *deps):
        before = queue[-DEPTH : len(queue) - DEPTH + 1] if len(queue) >= DEPTH else []
        queue.append(send(block, route, [*deps, *before]))
        return queue[-1]

    far_chips = list(range(chips - 1, 0, -1))
    near_routes = [(label, 0) for label in far_chips]
    far_routes = [(label, 1) for label in far_chips]
    near = send_blocks(m, g, workers, near_routes, [[0, rows]] * len(near_routes), [], "near")
    held = [queued(block, route) for route, block in zip(near_routes, near)]
    routes = far_routes + [(0, 1), (0, 0)]
    cuts = [cut] * len(far_routes) + [[0, rows]] * 2
    sends = send_blocks(m, g, workers, routes, cuts, near[:1], "far")
    held += [send(sends[-2], (0, 1)), sends[-1]]
    updated, own_w = update(m, g, w, workers, workers, sends[:1])
    got = [[], []]
    for part in range(2):
        for i, route in enumerate(far_routes):
            early = part == 0 and i < DEPTH - len(near_routes)
            got[part].append(queued(sends[2 * i + part], route, *([] if early else [own_w])))

    gathered = []
    for got, (low, high) in zip(got, parts):
        new = [trim(own_w, held + got, low, high, [], "trim")]
        for label in range(1, chips):
            step = 1 << label.bit_length() - 1
            if chips & (chips - 1) == 0:
                new.append(send(new[label - step], (step, 0)))
            else:
                new.append(send(new[0], (label, 0)))
        gathered.append(new)
    blocks = {}
    for new, (low, high) in zip(gathered, parts):
        for label, block in enumerate(new):
            blocks[low, label, 0] = block
            if low == 0:
                block = copied(block, [gathered[1][min(LATER, chips - 1)]])
            blocks[low, label, 1] = send(block, (0, 1))
    result = place(blocks, workers, rows)
    return updated.reshape(momentum.shape), result.reshape(weights.shape)


def solution(mesh):
    return jax.shard_map(
        body,
        mesh=mesh,
        in_specs=(P("worker", "shard"), P("worker", "shard"), P("shard")),
        out_specs=(P("worker", "shard"), P("shard")),
        check_vma=False,
    )
```

```python
import functools

import jax
import jax.numpy as jnp
from jax import lax
from jax.experimental import pallas as pl
from jax.experimental.pallas import tpu as pltpu
from jax.sharding import PartitionSpec as P

LANES = 128
DEPTH = 4
WAIT = 1
CORES = 2


def cost(size):
    return pl.CostEstimate(flops=size, bytes_accessed=4 * size, transcendentals=0)


ANY = pl.BlockSpec(memory_space=pl.ANY)
VMEM = pl.BlockSpec(memory_space=pltpu.VMEM)


def turned(label, core, chips):
    bits = chips.bit_length() - 1
    second = sum(1 << (j + 1) % bits for j in range(bits) if label >> j & 1) if bits else 0
    return label + core * (second - label)


def other_chip(chip, label, core, chips):
    if chips & (chips - 1) == 0:
        return chip ^ turned(label, core, chips)
    return (label - chip) % chips


def target(worker, label, flip, count):
    chip, core = worker // CORES, worker % CORES
    core_there = core + flip * (1 - 2 * core)
    return CORES * other_chip(chip, label, core, count // CORES) + core_there


def origin(worker, label, flip, count):
    chip, core = worker // CORES, worker % CORES
    core_there = core + flip * (1 - 2 * core)
    return CORES * other_chip(chip, label, core_there, count // CORES) + core_there


def block_of(worker, count):
    chips = count // CORES
    return (worker % CORES) * chips + worker // CORES


def order_pair(values, low, high):
    former, latter = values[low], values[high]
    values[low] = jnp.minimum(former, latter)
    values[high] = jnp.maximum(former, latter)


def network(count):
    pairs = []
    span = 1
    while span < count:
        step = span
        while step >= 1:
            for first in range(step % span, count - step, 2 * step):
                for low in range(first, min(first + step, count - step)):
                    if low // (2 * span) == (low + step) // (2 * span):
                        pairs.append((low, low + step))
            step //= 2
        span *= 2
    return pairs


def kept_mean(values):
    values = list(values)
    count = len(values)
    trim = count // 4
    for low, high in network(count):
        order_pair(values, low, high)
    total = functools.reduce(jnp.add, values[trim : count - trim])
    return total / (count - 2 * trim)


def send_kernel(workers, routes, cuts, rows, deps, m_ref, g_ref, *rest):
    rest = rest[deps:]
    count = sum(len(cut) - 1 for cut in cuts)
    sends = rest[:count]
    m_buf, g_buf, sem = rest[count:]
    me = lax.axis_index("worker")
    loads = []
    for i, route in enumerate(routes):
        start = pl.multiple_of(block_of(target(me, *route, workers), workers) * rows, 8)
        span = pl.ds(start, rows)
        pair = [
            pltpu.make_async_copy(m_ref.at[span], m_buf.at[i], sem.at[2 * i]),
            pltpu.make_async_copy(g_ref.at[span], g_buf.at[i], sem.at[2 * i + 1]),
        ]
        for copy in pair:
            copy.start()
        loads.append(pair)
    at = 0
    for i, cut in enumerate(cuts):
        for copy in loads[i]:
            copy.wait()
        for low, high in zip(cut[:-1], cut[1:]):
            sends[at][...] = 0.9 * m_buf[i, low:high] + g_buf[i, low:high]
            at += 1


def send_blocks(momentum, gradient, workers, routes, cuts, deps, name):
    rows = momentum.shape[0] // workers
    sizes = [high - low for cut in cuts for low, high in zip(cut[:-1], cut[1:])]
    return pl.pallas_call(
        functools.partial(send_kernel, workers, routes, cuts, rows, len(deps)),
        out_shape=[jax.ShapeDtypeStruct((size, LANES), jnp.float32) for size in sizes],
        in_specs=[ANY] * (2 + len(deps)),
        out_specs=[VMEM] * len(sizes),
        scratch_shapes=[
            pltpu.VMEM((len(routes), rows, LANES), jnp.float32),
            pltpu.VMEM((len(routes), rows, LANES), jnp.float32),
            pltpu.SemaphoreType.DMA((2 * len(routes),)),
        ],
        compiler_params=pltpu.CompilerParams(vmem_limit_bytes=16 << 20),
        cost_estimate=cost(3 * LANES * sum(sizes)),
        name=name,
    )(momentum, gradient, *deps)


def update_kernel(workers, pieces, rows, deps, m_ref, g_ref, w_ref, *rest):
    u_ref, own_ref, m_buf, g_buf, in_sem, out_sem, own_sem = rest[deps:]
    size = own_ref.shape[0]
    start = pl.multiple_of(block_of(lax.axis_index("worker"), workers) * size, 8)
    loads, stores = [], []
    for i in range(pieces):
        span = pl.ds(i * rows, rows)
        loads.append(
            [
                pltpu.make_async_copy(m_ref.at[span], m_buf.at[i], in_sem.at[2 * i]),
                pltpu.make_async_copy(g_ref.at[span], g_buf.at[i], in_sem.at[2 * i + 1]),
            ]
        )
        stores.append(pltpu.make_async_copy(g_buf.at[i], u_ref.at[span], out_sem.at[i]))
        for copy in loads[i]:
            copy.start()
    own = pltpu.make_async_copy(w_ref.at[pl.ds(start, size)], own_ref, own_sem)
    own.start()
    for i in range(pieces):
        for copy in loads[i]:
            copy.wait()
        g_buf[i] = 0.9 * m_buf[i] + g_buf[i]
        stores[i].start()
    for copy in stores + [own]:
        copy.wait()


def update(momentum, gradient, weights, workers, pieces, deps):
    rows = momentum.shape[0] // pieces
    own = (weights.shape[0] // workers, LANES)
    return pl.pallas_call(
        functools.partial(update_kernel, workers, pieces, rows, len(deps)),
        out_shape=[
            jax.ShapeDtypeStruct(momentum.shape, jnp.float32),
            jax.ShapeDtypeStruct(own, jnp.float32),
        ],
        in_specs=[ANY] * (3 + len(deps)),
        out_specs=[ANY, VMEM],
        scratch_shapes=[
            pltpu.VMEM((pieces, rows, LANES), jnp.float32),
            pltpu.VMEM((pieces, rows, LANES), jnp.float32),
            pltpu.SemaphoreType.DMA((2 * pieces,)),
            pltpu.SemaphoreType.DMA((pieces,)),
            pltpu.SemaphoreType.DMA,
        ],
        compiler_params=pltpu.CompilerParams(vmem_limit_bytes=16 << 20),
        cost_estimate=cost(3 * momentum.size),
        name="update",
    )(momentum, gradient, weights, *deps)


def trim_kernel(size, starts, *rest):
    blocks, o_ref = rest[: len(starts)], rest[-1]
    step = 8 * max(1, 32 // (len(starts) - 1))

    def one(i, carry):
        at = pl.multiple_of(i * step, step)
        own, *values = [b[pl.ds(s + at, step)] for b, s in zip(blocks, starts)]
        o_ref[pl.ds(at, step)] = own - 0.1 * kept_mean(values)
        return carry

    lax.fori_loop(0, size // step, one, 0)


def trim(weights, blocks, low, high, deps, name):
    rows = weights.shape[0]
    size = high - low
    starts = [low if block.shape[0] == rows else 0 for block in [weights, *blocks]]
    return pl.pallas_call(
        functools.partial(trim_kernel, size, starts),
        out_shape=jax.ShapeDtypeStruct((size, LANES), jnp.float32),
        in_specs=[VMEM] * len(starts) + [ANY] * len(deps),
        out_specs=VMEM,
        compiler_params=pltpu.CompilerParams(vmem_limit_bytes=16 << 20),
        cost_estimate=cost((len(starts) + 1) * size * LANES),
        name=name,
    )(weights, *blocks, *deps)


def place_kernel(workers, rows, places, *rest):
    blocks, (o_ref, sem) = rest[: len(places)], rest[len(places) :]
    me = lax.axis_index("worker")
    copies = []
    for i, (block, (low, *route)) in enumerate(zip(blocks, places)):
        start = block_of(origin(me, *route, workers), workers) * rows + low
        there = o_ref.at[pl.ds(pl.multiple_of(start, 8), block.shape[0])]
        copies.append(pltpu.make_async_copy(block, there, sem.at[i]))
        copies[i].start()
    for copy in copies:
        copy.wait()


def place(blocks, workers, rows):
    return pl.pallas_call(
        functools.partial(place_kernel, workers, rows, list(blocks)),
        out_shape=jax.ShapeDtypeStruct((workers * rows, LANES), jnp.float32),
        in_specs=[ANY] * len(blocks),
        out_specs=ANY,
        scratch_shapes=[pltpu.SemaphoreType.DMA((len(blocks),))],
        compiler_params=pltpu.CompilerParams(vmem_limit_bytes=16 << 20),
        cost_estimate=cost(2 * LANES * workers * rows),
        name="place",
    )(*blocks.values())


def gate_kernel(*refs):
    del refs


def gate(blocks, deps):
    return pl.pallas_call(
        gate_kernel,
        out_shape=[jax.ShapeDtypeStruct(b.shape, b.dtype) for b in blocks],
        in_specs=[ANY] * (len(blocks) + len(deps)),
        out_specs=[ANY] * len(blocks),
        input_output_aliases={i: i for i in range(len(blocks))},
        compiler_params=pltpu.CompilerParams(vmem_limit_bytes=1 << 20),
        name="gate",
    )(*blocks, *deps)


def in_hbm(array):
    return pltpu.with_memory_space_constraint(array.reshape(-1, LANES), pltpu.HBM)


def body(momentum, gradient, weights):
    workers = lax.axis_size("worker")
    chips = workers // CORES
    m, g, w = in_hbm(momentum), in_hbm(gradient), in_hbm(weights)
    rows = m.shape[0] // workers
    cut = [0, rows // 2, rows]
    parts = list(zip(cut[:-1], cut[1:]))
    queue = []

    def send(block, route, deps=()):
        if deps:
            (block,) = gate([block], list(deps))
        pairs = [(i, target(i, *route, workers)) for i in range(workers)]
        return lax.ppermute(block, "worker", pairs)

    def queued(block, route, *deps):
        before = queue[-DEPTH : len(queue) - DEPTH + 1] if len(queue) >= DEPTH else []
        queue.append(send(block, route, [*deps, *before]))
        return queue[-1]

    far_chips = list(range(chips - 1, 0, -1))
    near_routes = [(label, 0) for label in range(1, chips)]
    far_routes = [(label, 1) for label in far_chips]
    near = send_blocks(m, g, workers, near_routes, [[0, rows]] * len(near_routes), [], "near")
    held = [queued(block, route) for route, block in zip(near_routes, near)]
    routes = far_routes + [(0, 1), (0, 0)]
    cuts = [cut] * len(far_routes) + [[0, rows]] * 2
    sends = send_blocks(m, g, workers, routes, cuts, near[:1], "far")
    held += [send(sends[-2], (0, 1)), sends[-1]]
    updated, own_w = update(m, g, w, workers, workers, sends[:1])
    got = [[], []]
    for part in range(2):
        for i, route in enumerate(far_routes):
            early = part == 0 and i < DEPTH - len(near_routes)
            got[part].append(queued(sends[2 * i + part], route, *([] if early else [own_w])))

    gathered = []
    for part, (low, high) in enumerate(parts):
        deps = got[1][:WAIT] if part == 0 else []
        new = [trim(own_w, held + got[part], low, high, deps, "trim")]
        for label in range(1, chips):
            step = 1 << label.bit_length() - 1
            if chips & (chips - 1) == 0:
                new.append(send(new[label - step], (step, 0)))
            else:
                new.append(send(new[0], (label, 0)))
        gathered.append(new)
    blocks = {}
    for new, (low, high) in zip(gathered, parts):
        for label, block in enumerate(new):
            blocks[low, label, 0] = block
            blocks[low, label, 1] = send(block, (0, 1))
    result = place(blocks, workers, rows)
    return updated.reshape(momentum.shape), result.reshape(weights.shape)


def solution(mesh):
    return jax.shard_map(
        body,
        mesh=mesh,
        in_specs=(P("worker", "shard"), P("worker", "shard"), P("shard")),
        out_specs=(P("worker", "shard"), P("shard")),
        check_vma=False,
    )
```

```python
import functools

import jax
import jax.numpy as jnp
from jax import lax
from jax.experimental import pallas as pl
from jax.experimental.pallas import tpu as pltpu
from jax.sharding import PartitionSpec as P

LANES = 128
DEPTH = 4
WAIT = 1
LAST = 2
CORES = 2


def cost(size):
    return pl.CostEstimate(flops=size, bytes_accessed=4 * size, transcendentals=0)


ANY = pl.BlockSpec(memory_space=pl.ANY)
VMEM = pl.BlockSpec(memory_space=pltpu.VMEM)


def turned(label, core, chips):
    bits = chips.bit_length() - 1
    second = sum(1 << (j + 1) % bits for j in range(bits) if label >> j & 1) if bits else 0
    return label + core * (second - label)


def other_chip(chip, label, core, chips):
    if chips & (chips - 1) == 0:
        return chip ^ turned(label, core, chips)
    return (label - chip) % chips


def target(worker, label, flip, count):
    chip, core = worker // CORES, worker % CORES
    core_there = core + flip * (1 - 2 * core)
    return CORES * other_chip(chip, label, core, count // CORES) + core_there


def origin(worker, label, flip, count):
    chip, core = worker // CORES, worker % CORES
    core_there = core + flip * (1 - 2 * core)
    return CORES * other_chip(chip, label, core_there, count // CORES) + core_there


def block_of(worker, count):
    chips = count // CORES
    return (worker % CORES) * chips + worker // CORES


def order_pair(values, low, high):
    former, latter = values[low], values[high]
    values[low] = jnp.minimum(former, latter)
    values[high] = jnp.maximum(former, latter)


def network(count):
    pairs = []
    span = 1
    while span < count:
        step = span
        while step >= 1:
            for first in range(step % span, count - step, 2 * step):
                for low in range(first, min(first + step, count - step)):
                    if low // (2 * span) == (low + step) // (2 * span):
                        pairs.append((low, low + step))
            step //= 2
        span *= 2
    return pairs


def kept_mean(values):
    values = list(values)
    count = len(values)
    trim = count // 4
    for low, high in network(count):
        order_pair(values, low, high)
    total = functools.reduce(jnp.add, values[trim : count - trim])
    return total / (count - 2 * trim)


def send_kernel(workers, routes, cuts, rows, deps, m_ref, g_ref, *rest):
    rest = rest[deps:]
    count = sum(len(cut) - 1 for cut in cuts)
    sends = rest[:count]
    m_buf, g_buf, sem = rest[count:]
    me = lax.axis_index("worker")
    loads = []
    for i, route in enumerate(routes):
        start = pl.multiple_of(block_of(target(me, *route, workers), workers) * rows, 8)
        span = pl.ds(start, rows)
        pair = [
            pltpu.make_async_copy(m_ref.at[span], m_buf.at[i], sem.at[2 * i]),
            pltpu.make_async_copy(g_ref.at[span], g_buf.at[i], sem.at[2 * i + 1]),
        ]
        for copy in pair:
            copy.start()
        loads.append(pair)
    at = 0
    for i, cut in enumerate(cuts):
        for copy in loads[i]:
            copy.wait()
        for low, high in zip(cut[:-1], cut[1:]):
            sends[at][...] = 0.9 * m_buf[i, low:high] + g_buf[i, low:high]
            at += 1


def send_blocks(momentum, gradient, workers, routes, cuts, deps, name):
    rows = momentum.shape[0] // workers
    sizes = [high - low for cut in cuts for low, high in zip(cut[:-1], cut[1:])]
    return pl.pallas_call(
        functools.partial(send_kernel, workers, routes, cuts, rows, len(deps)),
        out_shape=[jax.ShapeDtypeStruct((size, LANES), jnp.float32) for size in sizes],
        in_specs=[ANY] * (2 + len(deps)),
        out_specs=[VMEM] * len(sizes),
        scratch_shapes=[
            pltpu.VMEM((len(routes), rows, LANES), jnp.float32),
            pltpu.VMEM((len(routes), rows, LANES), jnp.float32),
            pltpu.SemaphoreType.DMA((2 * len(routes),)),
        ],
        compiler_params=pltpu.CompilerParams(vmem_limit_bytes=16 << 20),
        cost_estimate=cost(3 * LANES * sum(sizes)),
        name=name,
    )(momentum, gradient, *deps)


def update_kernel(workers, pieces, rows, deps, m_ref, g_ref, w_ref, *rest):
    u_ref, own_ref, m_buf, g_buf, in_sem, out_sem, own_sem = rest[deps:]
    size = own_ref.shape[0]
    start = pl.multiple_of(block_of(lax.axis_index("worker"), workers) * size, 8)
    loads, stores = [], []
    for i in range(pieces):
        span = pl.ds(i * rows, rows)
        loads.append(
            [
                pltpu.make_async_copy(m_ref.at[span], m_buf.at[i], in_sem.at[2 * i]),
                pltpu.make_async_copy(g_ref.at[span], g_buf.at[i], in_sem.at[2 * i + 1]),
            ]
        )
        stores.append(pltpu.make_async_copy(g_buf.at[i], u_ref.at[span], out_sem.at[i]))
        for copy in loads[i]:
            copy.start()
    own = pltpu.make_async_copy(w_ref.at[pl.ds(start, size)], own_ref, own_sem)
    own.start()
    for i in range(pieces):
        for copy in loads[i]:
            copy.wait()
        g_buf[i] = 0.9 * m_buf[i] + g_buf[i]
        stores[i].start()
    for copy in stores + [own]:
        copy.wait()


def update(momentum, gradient, weights, workers, pieces, deps):
    rows = momentum.shape[0] // pieces
    own = (weights.shape[0] // workers, LANES)
    return pl.pallas_call(
        functools.partial(update_kernel, workers, pieces, rows, len(deps)),
        out_shape=[
            jax.ShapeDtypeStruct(momentum.shape, jnp.float32),
            jax.ShapeDtypeStruct(own, jnp.float32),
        ],
        in_specs=[ANY] * (3 + len(deps)),
        out_specs=[ANY, VMEM],
        scratch_shapes=[
            pltpu.VMEM((pieces, rows, LANES), jnp.float32),
            pltpu.VMEM((pieces, rows, LANES), jnp.float32),
            pltpu.SemaphoreType.DMA((2 * pieces,)),
            pltpu.SemaphoreType.DMA((pieces,)),
            pltpu.SemaphoreType.DMA,
        ],
        compiler_params=pltpu.CompilerParams(vmem_limit_bytes=16 << 20),
        cost_estimate=cost(3 * momentum.size),
        name="update",
    )(momentum, gradient, weights, *deps)


def trim_kernel(size, starts, *rest):
    blocks, o_ref = rest[: len(starts)], rest[-1]
    step = 8 * max(1, 32 // (len(starts) - 1))

    def one(i, carry):
        at = pl.multiple_of(i * step, step)
        own, *values = [b[pl.ds(s + at, step)] for b, s in zip(blocks, starts)]
        o_ref[pl.ds(at, step)] = own - 0.1 * kept_mean(values)
        return carry

    lax.fori_loop(0, size // step, one, 0)


def trim(weights, blocks, low, high, deps, name):
    rows = weights.shape[0]
    size = high - low
    starts = [low if block.shape[0] == rows else 0 for block in [weights, *blocks]]
    return pl.pallas_call(
        functools.partial(trim_kernel, size, starts),
        out_shape=jax.ShapeDtypeStruct((size, LANES), jnp.float32),
        in_specs=[VMEM] * len(starts) + [ANY] * len(deps),
        out_specs=VMEM,
        compiler_params=pltpu.CompilerParams(vmem_limit_bytes=16 << 20),
        cost_estimate=cost((len(starts) + 1) * size * LANES),
        name=name,
    )(weights, *blocks, *deps)


def place_kernel(workers, rows, places, count, *rest):
    blocks, (o_ref, sem) = rest[: len(places)], rest[count:]
    me = lax.axis_index("worker")
    copies = []
    for i, (block, (low, *route)) in enumerate(zip(blocks, places)):
        start = block_of(origin(me, *route, workers), workers) * rows + low
        there = o_ref.at[pl.ds(pl.multiple_of(start, 8), block.shape[0])]
        copies.append(pltpu.make_async_copy(block, there, sem.at[i]))
        copies[i].start()
    for copy in copies:
        copy.wait()


def place(blocks, workers, rows, into=()):
    operands = [*blocks.values(), *into]
    return pl.pallas_call(
        functools.partial(place_kernel, workers, rows, list(blocks), len(operands)),
        out_shape=jax.ShapeDtypeStruct((workers * rows, LANES), jnp.float32),
        in_specs=[ANY] * len(operands),
        out_specs=ANY,
        scratch_shapes=[pltpu.SemaphoreType.DMA((len(blocks),))],
        input_output_aliases={len(blocks): 0} if into else {},
        compiler_params=pltpu.CompilerParams(vmem_limit_bytes=16 << 20),
        cost_estimate=cost(2 * LANES * sum(block.shape[0] for block in blocks.values())),
        name="place",
    )(*operands)


def gate_kernel(*refs):
    del refs


def gate(blocks, deps):
    return pl.pallas_call(
        gate_kernel,
        out_shape=[jax.ShapeDtypeStruct(b.shape, b.dtype) for b in blocks],
        in_specs=[ANY] * (len(blocks) + len(deps)),
        out_specs=[ANY] * len(blocks),
        input_output_aliases={i: i for i in range(len(blocks))},
        compiler_params=pltpu.CompilerParams(vmem_limit_bytes=1 << 20),
        name="gate",
    )(*blocks, *deps)


def in_hbm(array):
    return pltpu.with_memory_space_constraint(array.reshape(-1, LANES), pltpu.HBM)


def body(momentum, gradient, weights):
    workers = lax.axis_size("worker")
    chips = workers // CORES
    m, g, w = in_hbm(momentum), in_hbm(gradient), in_hbm(weights)
    rows = m.shape[0] // workers
    cut = [0, rows // 2, rows]
    parts = list(zip(cut[:-1], cut[1:]))
    queue = []

    def send(block, route, deps=()):
        if deps:
            (block,) = gate([block], list(deps))
        pairs = [(i, target(i, *route, workers)) for i in range(workers)]
        return lax.ppermute(block, "worker", pairs)

    def queued(block, route, *deps):
        before = queue[-DEPTH : len(queue) - DEPTH + 1] if len(queue) >= DEPTH else []
        queue.append(send(block, route, [*deps, *before]))
        return queue[-1]

    far_chips = list(range(chips - 1, 0, -1))
    near_routes = [(label, 0) for label in range(1, chips)]
    far_routes = [(label, 1) for label in far_chips]
    near = []
    for group in (near_routes[:2], near_routes[2:]):
        spans = [[0, rows]] * len(group)
        blocks = send_blocks(m, g, workers, group, spans, near[:1], "near") if group else []
        near += blocks
    held = [queued(block, route) for route, block in zip(near_routes, near)]
    routes = far_routes + [(0, 1), (0, 0)]
    cuts = [cut] * len(far_routes) + [[0, rows]] * 2
    sends = send_blocks(m, g, workers, routes, cuts, near[:1], "far")
    held += [send(sends[-2], (0, 1)), sends[-1]]
    updated, own_w = update(m, g, w, workers, workers, sends[:1])
    got = [[], []]
    for part in range(2):
        for i, route in enumerate(far_routes):
            early = part == 0 and i < DEPTH - len(near_routes)
            got[part].append(queued(sends[2 * i + part], route, *([] if early else [own_w])))

    gathered = []
    for part, (low, high) in enumerate(parts):
        deps = got[1][:WAIT] if part == 0 else []
        new = [trim(own_w, held + got[part], low, high, deps, "trim")]
        for label in range(1, chips):
            step = 1 << label.bit_length() - 1
            if chips & (chips - 1) == 0:
                new.append(send(new[label - step], (step, 0)))
            else:
                new.append(send(new[0], (label, 0)))
        gathered.append(new)
    blocks = {}
    for new, (low, high) in zip(gathered, parts):
        for label, block in enumerate(new):
            blocks[low, label, 0] = block
            blocks[low, label, 1] = send(block, (0, 1))
    last = list(blocks)[-LAST:]
    result = place({k: v for k, v in blocks.items() if k not in last}, workers, rows)
    result = place({k: blocks[k] for k in last}, workers, rows, [result])
    return updated.reshape(momentum.shape), result.reshape(weights.shape)


def solution(mesh):
    return jax.shard_map(
        body,
        mesh=mesh,
        in_specs=(P("worker", "shard"), P("worker", "shard"), P("shard")),
        out_specs=(P("worker", "shard"), P("shard")),
        check_vma=False,
    )
```

```python
import functools

import jax
import jax.numpy as jnp
from jax import lax
from jax.experimental import pallas as pl
from jax.experimental.pallas import tpu as pltpu
from jax.sharding import PartitionSpec as P

LANES = 128
DEPTH = 4
EARLY = 2
WAIT = 1
LAST = 2
CORES = 2


def cost(size):
    return pl.CostEstimate(flops=size, bytes_accessed=4 * size, transcendentals=0)


ANY = pl.BlockSpec(memory_space=pl.ANY)
VMEM = pl.BlockSpec(memory_space=pltpu.VMEM)


def turned(label, core, chips):
    bits = chips.bit_length() - 1
    second = sum(1 << (j + 1) % bits for j in range(bits) if label >> j & 1) if bits else 0
    return label + core * (second - label)


def other_chip(chip, label, core, chips):
    if chips & (chips - 1) == 0:
        return chip ^ turned(label, core, chips)
    return (label - chip) % chips


def target(worker, label, flip, count):
    chip, core = worker // CORES, worker % CORES
    core_there = core + flip * (1 - 2 * core)
    return CORES * other_chip(chip, label, core, count // CORES) + core_there


def origin(worker, label, flip, count):
    chip, core = worker // CORES, worker % CORES
    core_there = core + flip * (1 - 2 * core)
    return CORES * other_chip(chip, label, core_there, count // CORES) + core_there


def block_of(worker, count):
    chips = count // CORES
    return (worker % CORES) * chips + worker // CORES


def order_pair(values, low, high):
    former, latter = values[low], values[high]
    values[low] = jnp.minimum(former, latter)
    values[high] = jnp.maximum(former, latter)


def network(count):
    pairs = []
    span = 1
    while span < count:
        step = span
        while step >= 1:
            for first in range(step % span, count - step, 2 * step):
                for low in range(first, min(first + step, count - step)):
                    if low // (2 * span) == (low + step) // (2 * span):
                        pairs.append((low, low + step))
            step //= 2
        span *= 2
    return pairs


def kept_mean(values):
    values = list(values)
    count = len(values)
    trim = count // 4
    for low, high in network(count):
        order_pair(values, low, high)
    total = functools.reduce(jnp.add, values[trim : count - trim])
    return total / (count - 2 * trim)


def send_kernel(workers, routes, cuts, rows, deps, m_ref, g_ref, *rest):
    rest = rest[deps:]
    count = sum(len(cut) - 1 for cut in cuts)
    sends = rest[:count]
    m_buf, g_buf, sem = rest[count:]
    me = lax.axis_index("worker")
    loads = []
    for i, route in enumerate(routes):
        start = pl.multiple_of(block_of(target(me, *route, workers), workers) * rows, 8)
        span = pl.ds(start, rows)
        pair = [
            pltpu.make_async_copy(m_ref.at[span], m_buf.at[i], sem.at[2 * i]),
            pltpu.make_async_copy(g_ref.at[span], g_buf.at[i], sem.at[2 * i + 1]),
        ]
        for copy in pair:
            copy.start()
        loads.append(pair)
    at = 0
    for i, cut in enumerate(cuts):
        for copy in loads[i]:
            copy.wait()
        for low, high in zip(cut[:-1], cut[1:]):
            sends[at][...] = 0.9 * m_buf[i, low:high] + g_buf[i, low:high]
            at += 1


def send_blocks(momentum, gradient, workers, routes, cuts, deps, name):
    rows = momentum.shape[0] // workers
    sizes = [high - low for cut in cuts for low, high in zip(cut[:-1], cut[1:])]
    return pl.pallas_call(
        functools.partial(send_kernel, workers, routes, cuts, rows, len(deps)),
        out_shape=[jax.ShapeDtypeStruct((size, LANES), jnp.float32) for size in sizes],
        in_specs=[ANY] * (2 + len(deps)),
        out_specs=[VMEM] * len(sizes),
        scratch_shapes=[
            pltpu.VMEM((len(routes), rows, LANES), jnp.float32),
            pltpu.VMEM((len(routes), rows, LANES), jnp.float32),
            pltpu.SemaphoreType.DMA((2 * len(routes),)),
        ],
        compiler_params=pltpu.CompilerParams(vmem_limit_bytes=16 << 20),
        cost_estimate=cost(3 * LANES * sum(sizes)),
        name=name,
    )(momentum, gradient, *deps)


def update_kernel(workers, pieces, rows, deps, m_ref, g_ref, w_ref, *rest):
    u_ref, own_ref, m_buf, g_buf, in_sem, out_sem, own_sem = rest[deps:]
    size = own_ref.shape[0]
    start = pl.multiple_of(block_of(lax.axis_index("worker"), workers) * size, 8)
    loads, stores = [], []
    for i in range(pieces):
        span = pl.ds(i * rows, rows)
        loads.append(
            [
                pltpu.make_async_copy(m_ref.at[span], m_buf.at[i], in_sem.at[2 * i]),
                pltpu.make_async_copy(g_ref.at[span], g_buf.at[i], in_sem.at[2 * i + 1]),
            ]
        )
        stores.append(pltpu.make_async_copy(g_buf.at[i], u_ref.at[span], out_sem.at[i]))
        for copy in loads[i]:
            copy.start()
    own = pltpu.make_async_copy(w_ref.at[pl.ds(start, size)], own_ref, own_sem)
    own.start()
    for i in range(pieces):
        for copy in loads[i]:
            copy.wait()
        g_buf[i] = 0.9 * m_buf[i] + g_buf[i]
        stores[i].start()
    for copy in stores + [own]:
        copy.wait()


def update(momentum, gradient, weights, workers, pieces, deps):
    rows = momentum.shape[0] // pieces
    own = (weights.shape[0] // workers, LANES)
    return pl.pallas_call(
        functools.partial(update_kernel, workers, pieces, rows, len(deps)),
        out_shape=[
            jax.ShapeDtypeStruct(momentum.shape, jnp.float32),
            jax.ShapeDtypeStruct(own, jnp.float32),
        ],
        in_specs=[ANY] * (3 + len(deps)),
        out_specs=[ANY, VMEM],
        scratch_shapes=[
            pltpu.VMEM((pieces, rows, LANES), jnp.float32),
            pltpu.VMEM((pieces, rows, LANES), jnp.float32),
            pltpu.SemaphoreType.DMA((2 * pieces,)),
            pltpu.SemaphoreType.DMA((pieces,)),
            pltpu.SemaphoreType.DMA,
        ],
        compiler_params=pltpu.CompilerParams(vmem_limit_bytes=16 << 20),
        cost_estimate=cost(3 * momentum.size),
        name="update",
    )(momentum, gradient, weights, *deps)


def trim_kernel(size, starts, *rest):
    blocks, o_ref = rest[: len(starts)], rest[-1]
    step = 8 * max(1, 32 // (len(starts) - 1))

    def one(i, carry):
        at = pl.multiple_of(i * step, step)
        own, *values = [b[pl.ds(s + at, step)] for b, s in zip(blocks, starts)]
        o_ref[pl.ds(at, step)] = own - 0.1 * kept_mean(values)
        return carry

    lax.fori_loop(0, size // step, one, 0)


def trim(weights, blocks, low, high, deps, name):
    rows = weights.shape[0]
    size = high - low
    starts = [low if block.shape[0] == rows else 0 for block in [weights, *blocks]]
    return pl.pallas_call(
        functools.partial(trim_kernel, size, starts),
        out_shape=jax.ShapeDtypeStruct((size, LANES), jnp.float32),
        in_specs=[VMEM] * len(starts) + [ANY] * len(deps),
        out_specs=VMEM,
        compiler_params=pltpu.CompilerParams(vmem_limit_bytes=16 << 20),
        cost_estimate=cost((len(starts) + 1) * size * LANES),
        name=name,
    )(weights, *blocks, *deps)


def place_kernel(workers, rows, places, count, *rest):
    blocks, (o_ref, sem) = rest[: len(places)], rest[count:]
    me = lax.axis_index("worker")
    copies = []
    for i, (block, (low, *route)) in enumerate(zip(blocks, places)):
        start = block_of(origin(me, *route, workers), workers) * rows + low
        there = o_ref.at[pl.ds(pl.multiple_of(start, 8), block.shape[0])]
        copies.append(pltpu.make_async_copy(block, there, sem.at[i]))
        copies[i].start()
    for copy in copies:
        copy.wait()


def place(blocks, workers, rows, into=()):
    operands = [*blocks.values(), *into]
    return pl.pallas_call(
        functools.partial(place_kernel, workers, rows, list(blocks), len(operands)),
        out_shape=jax.ShapeDtypeStruct((workers * rows, LANES), jnp.float32),
        in_specs=[ANY] * len(operands),
        out_specs=ANY,
        scratch_shapes=[pltpu.SemaphoreType.DMA((len(blocks),))],
        input_output_aliases={len(blocks): 0} if into else {},
        compiler_params=pltpu.CompilerParams(vmem_limit_bytes=16 << 20),
        cost_estimate=cost(2 * LANES * sum(block.shape[0] for block in blocks.values())),
        name="place",
    )(*operands)


def gate_kernel(*refs):
    del refs


def gate(blocks, deps):
    return pl.pallas_call(
        gate_kernel,
        out_shape=[jax.ShapeDtypeStruct(b.shape, b.dtype) for b in blocks],
        in_specs=[ANY] * (len(blocks) + len(deps)),
        out_specs=[ANY] * len(blocks),
        input_output_aliases={i: i for i in range(len(blocks))},
        compiler_params=pltpu.CompilerParams(vmem_limit_bytes=1 << 20),
        name="gate",
    )(*blocks, *deps)


def in_hbm(array):
    return pltpu.with_memory_space_constraint(array.reshape(-1, LANES), pltpu.HBM)


def body(momentum, gradient, weights):
    workers = lax.axis_size("worker")
    chips = workers // CORES
    m, g, w = in_hbm(momentum), in_hbm(gradient), in_hbm(weights)
    rows = m.shape[0] // workers
    cut = [0, rows // 2, rows]
    parts = list(zip(cut[:-1], cut[1:]))
    queue = []

    def send(block, route, deps=()):
        if deps:
            (block,) = gate([block], list(deps))
        pairs = [(i, target(i, *route, workers)) for i in range(workers)]
        return lax.ppermute(block, "worker", pairs)

    def queued(block, route, *deps):
        before = queue[-DEPTH : len(queue) - DEPTH + 1] if len(queue) >= DEPTH else []
        queue.append(send(block, route, [*deps, *before]))
        return queue[-1]

    far_chips = list(range(chips - 1, 0, -1))
    near_routes = [(label, 0) for label in range(1, chips)]
    far_routes = [(label, 1) for label in far_chips]
    near = []
    for group in (near_routes[:2], near_routes[2:]):
        spans = [[0, rows]] * len(group)
        blocks = send_blocks(m, g, workers, group, spans, near[:1], "near") if group else []
        near += blocks
    held = [queued(block, route) for route, block in zip(near_routes, near)]
    routes = far_routes + [(0, 1), (0, 0)]
    cuts = [cut] * len(far_routes) + [[0, rows]] * 2
    sends = send_blocks(m, g, workers, routes, cuts, near[:1], "far")
    held += [send(sends[-2], (0, 1)), sends[-1]]
    updated, own_w = update(m, g, w, workers, workers, sends[:1])
    got = [[], []]
    for part in range(2):
        for i, route in enumerate(far_routes):
            early = part == 0 and i < EARLY
            got[part].append(queued(sends[2 * i + part], route, *([] if early else [own_w])))

    gathered = []
    for part, (low, high) in enumerate(parts):
        deps = got[1][:WAIT] if part == 0 else []
        new = [trim(own_w, held + got[part], low, high, deps, "trim")]
        for label in range(1, chips):
            step = 1 << label.bit_length() - 1
            if chips & (chips - 1) == 0:
                new.append(send(new[label - step], (step, 0)))
            else:
                new.append(send(new[0], (label, 0)))
        gathered.append(new)
    blocks = {}
    for new, (low, high) in zip(gathered, parts):
        for label, block in enumerate(new):
            blocks[low, label, 0] = block
            blocks[low, label, 1] = send(block, (0, 1))
    last = list(blocks)[-LAST:]
    result = place({k: v for k, v in blocks.items() if k not in last}, workers, rows)
    result = place({k: blocks[k] for k in last}, workers, rows, [result])
    return updated.reshape(momentum.shape), result.reshape(weights.shape)


def solution(mesh):
    return jax.shard_map(
        body,
        mesh=mesh,
        in_specs=(P("worker", "shard"), P("worker", "shard"), P("shard")),
        out_specs=(P("worker", "shard"), P("shard")),
        check_vma=False,
    )
```
